32 devices in a mesh: req: 16 (over z, y, x), ctx: 2 (over core).
Axes of the slice: x: 2, y: 2, z: 4, core: 2. Of those that a mesh axis runs over, the one named last changes fastest.
Arguments:
- conv_input: bfloat16 [16, 512, 10240], P('req', 'ctx'), may hold values from -6 to 6
- gate_input: bfloat16 [16, 512, 8192], P('req', 'ctx'), may hold values from -6 to 6
- dt_raw: bfloat16 [16, 512, 128], P('req', 'ctx'), may hold values from -3 to 3
- conv_weight: float32 [4, 10240], replicated, may hold values from -3 to 3
- conv_bias: float32 [10240], replicated, may hold values from -3 to 3
- dt_bias: float32 [128], replicated
- a_log: float32 [128], replicated
- d_skip: float32 [128], replicated, may hold values from 0.5 to 2
- norm_weight: float32 [8192], replicated, may hold values from 0.5 to 1.5
- conv_cache: bfloat16 [16, 3, 10240], P('req'), may hold values from -6 to 6
- state_pool: float32 [1024, 256, 128], P(('req', 'ctx')), may hold values from -6 to 6
- page_owner: int32 [16, 32], replicated, may hold values from 0 to 31, as said below
- page_slot: int32 [16, 32], replicated, may hold values from 0 to 31, as said below
- prefix_len: int32 [16], replicated, may hold values from 0 to 32767, as said below
- new_count: int32 [16], replicated, may hold values from 64 to 512, as said below
Outputs:
- mixed: bfloat16 [16, 512, 8192], P('req', 'ctx')
- new_conv: bfloat16 [16, 3, 10240], P('req')
- new_pool: float32 [1024, 256, 128], P(('req', 'ctx'))
The draws below stay inside these ranges and needn't reach their ends.
Inputs may be any that keep to these rules, and one draw needn't show every extreme that they name: `page_owner`: page j of request r holds rows j * 256 to (j + 1) * 256 - 1 of its state; devices are counted as req index times the ctx axis's size plus ctx index. The 16 pages j of one request with the same j // 16 lie on different devices, and every device holds exactly 16 pages of all requests together. `page_slot`: the pages held by one device lie in different slots; other slots hold nothing of these requests. `prefix_len`: some request has prefix length 0 in every draw. `new_count`: both ends are reached in every draw; the new tokens of a request fill its first slots.
All inputs are finite; a program needn't handle non-finite values.
Results may differ from the reference program's by a relative error of at most 0.0095.
Values may be sent and summed in bfloat16 or wider, within the bound.
A program may use at most 192 MiB of HBM per device.

```python
import math
import jax
import jax.numpy as jnp
from jax import lax

HEADS = 128
HDIM = 64
NSTATE = 128
GROUPS = 8
KCONV = 4
TOK_DEV = 256
INNER = 8192
CONVDIM = 10240
LEN = 512
REQS = 16
PPD = 16
PAGES = 32
PAGE_ROWS = 256
POOL_DEV = 32
SLOTS = 1024
N_REQ = 16
N_CTX = 2


def page_tables(key):
    base = jax.random.fold_in(key, 11)
    keys = jax.random.split(base, 4)
    devices = N_REQ * N_CTX
    sigma = jax.random.permutation(keys[0], devices)
    tau = jax.random.permutation(keys[1], devices)
    offsets = jax.random.permutation(keys[2], devices)[:PPD]
    position = (tau[:, None] + offsets[None, :]) % devices
    owner = sigma[position]
    slot_keys = jax.random.split(keys[3], devices)
    orders = jax.vmap(lambda single: jax.random.permutation(single, POOL_DEV))(slot_keys)
    slot = orders[owner, jnp.arange(PPD, dtype=jnp.int32)[None, :]]
    return (owner.reshape(N_REQ, PAGES).astype(jnp.int32), slot.reshape(N_REQ, PAGES).astype(jnp.int32))


def draw_page_owner(key, part):
    return page_tables(key)[0]


def draw_page_slot(key, part):
    return page_tables(key)[1]


def head_rates(key):
    base = jax.random.fold_in(key, 41)
    keys = jax.random.split(base, 4)
    target = jnp.exp(jax.random.uniform(keys[0], (HEADS,), jnp.float32, math.log(0.01), math.log(0.1)))
    share = 0.5
    slow = jax.random.uniform(keys[1], (HEADS,), jnp.float32) < share
    slow_rate = jnp.exp(jax.random.uniform(keys[2], (HEADS,), jnp.float32, jnp.log(0.3 / LEN), jnp.log(1.5 / LEN)))
    fast_rate = jnp.exp(jax.random.uniform(keys[3], (HEADS,), jnp.float32, math.log(1.0 / 50.0), math.log(1.0 / 30.0)))
    return (target, jnp.where(slow, slow_rate, fast_rate))


def draw_dt_bias(key, part):
    target, rate = head_rates(key)
    return jnp.log(jnp.expm1(target)).astype(jnp.float32)


def draw_a_log(key, part):
    target, rate = head_rates(key)
    return jnp.log(rate / target).astype(jnp.float32)


def draw_prefix_len(key, part):
    keys = jax.random.split(jax.random.fold_in(key, 23), 4)
    coin = jax.random.randint(keys[0], (REQS,), 0, 4) == 0
    small = jax.random.randint(keys[1], (REQS,), 0, 3)
    large = jax.random.randint(keys[2], (REQS,), 3, 32768)
    values = jnp.where(coin, small, large)
    order = jax.random.permutation(keys[3], REQS)
    values = values.at[order[0]].set(0).at[order[1]].set(32767)
    return values.astype(jnp.int32)


def draw_new_count(key, part):
    keys = jax.random.split(jax.random.fold_in(key, 29), 2)
    lowest = max(LEN // 8, KCONV)
    values = jax.random.randint(keys[0], (REQS,), lowest, LEN + 1)
    order = jax.random.permutation(keys[1], REQS)
    values = values.at[order[0]].set(LEN).at[order[1]].set(lowest)
    return values.astype(jnp.int32)


def block_scale(own_key, extent, cuts, smallest, top_value):
    loudness = 1.0
    for dim, blocks in cuts:
        heights = jax.random.uniform(jax.random.fold_in(jax.random.fold_in(own_key, 6), dim), (blocks,), jnp.float32, smallest / len(cuts), top_value / len(cuts))
        loudness = loudness * jnp.repeat(jnp.exp(heights), extent[dim] // blocks).reshape((-1,) + (1,) * (len(extent) - 1 - dim))
    return loudness


def centred(key, shape, scale, limit, pieces=(), held_as=jnp.bfloat16):
    drawn = jax.random.normal(key, shape, jnp.float32) * scale
    if len(pieces) > 0:
        drawn = block_scale(key, shape, pieces, -0.22, 0.18) * drawn
    return jnp.clip(drawn, min=-limit, max=limit).astype(held_as)


def setup_inputs(seed: int = 0) -> dict:
    arg_keys = jax.random.split(jax.random.key(seed), 16)
    return {
        "conv_input": centred(arg_keys[0], (REQS, LEN, CONVDIM), 1.0, 6.0, ((0, 16), (1, 2))),
        "gate_input": centred(arg_keys[1], (REQS, LEN, INNER), 1.0, 6.0, ((0, 16), (1, 2))),
        "dt_raw": centred(arg_keys[2], (REQS, LEN, HEADS), 0.5, 3.0, ((0, 16), (1, 2))),
        "conv_weight": centred(arg_keys[3], (KCONV, CONVDIM), KCONV ** -0.5, 3.0, (), jnp.float32),
        "conv_bias": centred(arg_keys[4], (CONVDIM,), 0.5, 3.0, (), jnp.float32),
        "dt_bias": draw_dt_bias(jax.random.fold_in(arg_keys[15], 71), 0),
        "a_log": draw_a_log(jax.random.fold_in(arg_keys[15], 71), 0),
        "d_skip": jnp.clip(jax.random.uniform(arg_keys[7], (HEADS,), jnp.float32, 0.5, 2.0), 0.5, 2.0),
        "norm_weight": jnp.clip(1.0 + 0.1 * jax.random.normal(arg_keys[8], (INNER,), jnp.float32), 0.5, 1.5),
        "conv_cache": centred(arg_keys[9], (REQS, KCONV - 1, CONVDIM), 1.0, 6.0, ((0, 16),)),
        "state_pool": centred(arg_keys[10], (SLOTS, PAGE_ROWS, NSTATE), 1.0, 6.0, ((0, 32),), jnp.float32),
        "page_owner": draw_page_owner(jax.random.fold_in(arg_keys[15], 71), 0),
        "page_slot": draw_page_slot(jax.random.fold_in(arg_keys[15], 71), 0),
        "prefix_len": draw_prefix_len(jax.random.fold_in(arg_keys[15], 71), 0),
        "new_count": draw_new_count(jax.random.fold_in(arg_keys[15], 71), 0),
    }


def conv_silu(extended, conv_weight, conv_bias, count_rows):
    accum = jnp.broadcast_to(conv_bias, (count_rows, conv_bias.shape[0])).astype(jnp.float32)
    for tap in range(conv_weight.shape[0]):
        accum = accum + conv_weight[tap] * extended[tap:tap + count_rows].astype(jnp.float32)
    return jax.nn.silu(accum).astype(jnp.bfloat16)

def local_block(inputs, b_proj, c_proj, step_size, log_decay):
    rows, heads, width = inputs.shape
    groups = b_proj.shape[1]
    per_group = heads // groups
    cumulative = jnp.cumsum(log_decay, axis=0)
    lower = jnp.arange(rows, dtype=jnp.int32)[:, None] >= jnp.arange(rows, dtype=jnp.int32)[None, :]
    grouped_x = jnp.moveaxis(inputs.reshape(rows, groups, per_group, width), 1, 0)
    grouped_cum = jnp.moveaxis(cumulative.reshape(rows, groups, per_group), 1, 0)
    grouped_dt = jnp.moveaxis(step_size.reshape(rows, groups, per_group), 1, 0)

    def per_head_group(items):
        x_grp, b_grp, c_grp, cum_grp, dt_grp = items
        scores = jnp.dot(c_grp, b_grp.T, preferred_element_type=jnp.float32)
        gap = cum_grp.T[:, :, None] - cum_grp.T[:, None, :]
        decay = jnp.where(lower, jnp.exp(jnp.where(lower, gap, 0.0)), 0.0)
        weights = lax.optimization_barrier((scores[None] * decay * dt_grp.T[:, None, :]).astype(jnp.bfloat16))
        intra = jnp.einsum('hts,shp->thp', weights.astype(jnp.float32), x_grp.astype(jnp.float32), precision=lax.Precision.HIGHEST)
        ending = jnp.exp(cum_grp[-1][None, :] - cum_grp) * dt_grp
        scaled = lax.optimization_barrier((x_grp.astype(jnp.float32) * ending[:, :, None]).astype(jnp.bfloat16))
        state = jnp.einsum('shp,sn->hpn', scaled.astype(jnp.float32), b_grp.astype(jnp.float32), precision=lax.Precision.HIGHEST)
        return (intra, state)
    intra, states = lax.map(per_head_group, (grouped_x, jnp.moveaxis(b_proj, 1, 0), jnp.moveaxis(c_proj, 1, 0), grouped_cum, grouped_dt))
    intra = jnp.moveaxis(intra, 0, 1).reshape(rows, heads, width)
    return (intra, states.reshape(heads, width, -1), cumulative)

def state_part(c_proj, cumulative, state):
    rows, groups, _ = c_proj.shape
    heads = cumulative.shape[1]
    rounded = lax.optimization_barrier(state.astype(jnp.bfloat16)).reshape(groups, -1, state.shape[2])
    product = jnp.einsum('tgn,gkn->tgk', c_proj.astype(jnp.float32), rounded.astype(jnp.float32), precision=lax.Precision.HIGHEST)
    return product.reshape(rows, heads, -1) * jnp.exp(cumulative)[:, :, None]

def finish(mixer, inputs, gate_in, d_skip, norm_weight, live, groups):
    rows = mixer.shape[0]
    summed = mixer + d_skip[None, :, None] * inputs.astype(jnp.float32)
    gated = summed.reshape(rows, -1) * jax.nn.silu(gate_in.astype(jnp.float32))
    grouped = gated.reshape(rows, groups, -1)
    factor = lax.rsqrt(lax.optimization_barrier(jnp.mean(grouped * grouped, axis=-1, keepdims=True)) + 1e-05)
    normed = (grouped * factor).reshape(rows, -1) * norm_weight
    return jnp.where(live[:, None], normed, 0.0).astype(jnp.bfloat16)

def reference(conv_input, gate_input, dt_raw, conv_weight, conv_bias, dt_bias, a_log, d_skip, norm_weight, conv_cache, state_pool, page_owner, page_slot, prefix_len, new_count):
    decay_rate = -jnp.exp(a_log)
    rim = KCONV - 1
    blocks = LEN // TOK_DEV
    global_slot = (page_owner * POOL_DEV + page_slot).astype(jnp.int32)

    def one_request(request):
        tokens = conv_input[request]
        prefix = prefix_len[request]
        count = new_count[request]
        keep_rows = jnp.arange(rim, dtype=jnp.int32) >= rim - prefix
        cached = jnp.where(keep_rows[:, None], conv_cache[request], jnp.zeros_like(conv_cache[request]))
        extended = jnp.concatenate([cached, tokens], axis=0)
        active = conv_silu(extended, conv_weight, conv_bias, LEN)
        inputs = active[:, :INNER].reshape(LEN, HEADS, HDIM)
        b_proj = active[:, INNER:INNER + GROUPS * NSTATE].reshape(LEN, GROUPS, NSTATE)
        c_proj = active[:, INNER + GROUPS * NSTATE:].reshape(LEN, GROUPS, NSTATE)
        live = jnp.arange(LEN, dtype=jnp.int32) < count
        step_size = jax.nn.softplus(dt_raw[request].astype(jnp.float32) + dt_bias) * live[:, None].astype(jnp.float32)
        log_decay = step_size * decay_rate
        initial = state_pool[global_slot[request]].reshape(HEADS, HDIM, NSTATE) * (prefix > 0).astype(jnp.float32)

        def per_block(state, items):
            x_blk, b_blk, c_blk, dt_blk, la_blk, gate_blk, live_blk = items
            intra, local_state, cumulative = local_block(x_blk, b_blk, c_blk, dt_blk, la_blk)
            carried = state_part(c_blk, cumulative, state)
            output = finish(intra + carried, x_blk, gate_blk, d_skip, norm_weight, live_blk, GROUPS)
            following = jnp.exp(cumulative[-1])[:, None, None] * state + local_state
            return (following, output)

        def blocked(array):
            return array.reshape((blocks, TOK_DEV) + array.shape[1:])
        final, outputs = lax.scan(per_block, initial, (blocked(inputs), blocked(b_proj), blocked(c_proj), blocked(step_size), blocked(log_decay), blocked(gate_input[request]), blocked(live)))
        tail = lax.dynamic_slice_in_dim(tokens, (count - rim).astype(jnp.int32), rim, 0)
        return (outputs.reshape(LEN, INNER), tail, final)
    mixed, tails, finals = lax.map(one_request, jnp.arange(REQS, dtype=jnp.int32))
    pages = finals.reshape(REQS * PAGES, PAGE_ROWS, NSTATE)
    new_pool = state_pool.at[global_slot.reshape(-1)].set(pages)
    return (mixed, tails, new_pool)
```

```python
import functools

import jax
import jax.numpy as jnp
from jax import lax
from jax.experimental import pallas as pl
from jax.experimental.pallas import tpu as pltpu
from jax.sharding import PartitionSpec as P

GROUPS = 8
F32 = jnp.float32
BF16 = jnp.bfloat16
NT = (((1,), (1,)), ((), ()))
TN = (((0,), (0,)), ((), ()))


def params(mib):
    return pltpu.CompilerParams(vmem_limit_bytes=mib * 1024 * 1024)


def cost(flops, moved):
    return pl.CostEstimate(flops=flops, bytes_accessed=moved, transcendentals=0)


def fetch_kernel(slots, pool, out):
    first = pl.program_id(0) * out.shape[0]

    def one(i, carry):
        out[i] = pool[slots[first + i]].astype(BF16)
        return carry

    lax.fori_loop(0, out.shape[0], one, 0)


def fetch_pages(pool, slots):
    count = slots.shape[0]
    steps = 4
    return pl.pallas_call(
        fetch_kernel,
        grid_spec=pltpu.PrefetchScalarGridSpec(
            num_scalar_prefetch=1,
            grid=(steps,),
            in_specs=[pl.BlockSpec(pool.shape, lambda i, s: (0, 0, 0))],
            out_specs=pl.BlockSpec((count // steps,) + pool.shape[1:], lambda i, s: (i, 0, 0)),
        ),
        out_shape=jax.ShapeDtypeStruct((count,) + pool.shape[1:], BF16),
        compiler_params=params(32),
        cost_estimate=cost(0, 6 * 2**20),
        name="fetch_pages",
    )(slots, pool)


def block_kernel(
    xin, bin_, cin, rimx, rimb, rimc, wx, wb, wc, ax, ab, ac, cl, clt, dtt, end, skip,
    y_ref, st_ref, c_ref, ext,
):
    rows, wide = xin.shape[1:]
    nstate = bin_.shape[2]
    taps = wx.shape[0]
    pad = rimx.shape[0]
    half = rows // 2
    for at, body, rim in ((0, xin, rimx), (wide, bin_, rimb), (wide + nstate, cin, rimc)):
        size = body.shape[2]
        ext[0:pad, at : at + size] = rim[...]
        ext[pad : pad + rows, at : at + size] = body[0].astype(F32)

    def act(at, col, size, weight, bias):
        accum = jnp.broadcast_to(bias[:, col : col + size], (rows, size))
        for k in range(taps):
            start = pad - taps + 1 + k
            piece = ext[start : start + rows, at + col : at + col + size]
            accum = accum + weight[k : k + 1, col : col + size] * piece
        return jax.nn.silu(accum).astype(BF16)

    b = act(wide, 0, nstate, wb, ab)
    c = act(wide + nstate, 0, nstate, wc, ac)
    c_ref[...] = c
    scores = lax.dot_general(c, b, NT, preferred_element_type=F32)
    row_id = lax.broadcasted_iota(jnp.int32, (half, half), 0)
    col_id = lax.broadcasted_iota(jnp.int32, (half, half), 1)
    lower = row_id >= col_id
    left = lax.broadcasted_iota(jnp.int32, (half, 128), 1) < 64
    left_all = lax.broadcasted_iota(jnp.int32, (rows, 128), 1) < 64
    for pair in range(wide // 128):
        cols = slice(pair * 128, pair * 128 + 128)
        x = act(0, pair * 128, 128, wx, ax)
        xf = x.astype(F32)
        tops, bottoms = [], []
        for head in (2 * pair, 2 * pair + 1):
            down = cl[0, :, head : head + 1]
            across = clt[head : head + 1, :]
            dt = dtt[head : head + 1, :]

            def part(r, s, diagonal):
                gap = down[r * half : (r + 1) * half] - across[:, s * half : (s + 1) * half]
                if diagonal:
                    gap = jnp.where(lower, gap, -1e30)
                value = scores[r * half : (r + 1) * half, s * half : (s + 1) * half] * jnp.exp(gap)
                return (value * dt[:, s * half : (s + 1) * half]).astype(BF16)

            tops.append(jnp.dot(part(0, 0, True), x[:half], preferred_element_type=F32))
            low = jnp.concatenate([part(1, 0, False), part(1, 1, True)], axis=1)
            bottoms.append(jnp.dot(low, x, preferred_element_type=F32))
        y_ref[0:half, cols] = jnp.where(left, tops[0], tops[1]) + skip[:, cols] * xf[:half]
        y_ref[half:rows, cols] = jnp.where(left, bottoms[0], bottoms[1]) + skip[:, cols] * xf[half:]
        ending = jnp.where(
            left_all, end[0, :, 2 * pair : 2 * pair + 1], end[0, :, 2 * pair + 1 : 2 * pair + 2]
        )
        scaled = (xf * ending).astype(BF16)
        st_ref[pair * 128 : pair * 128 + 128, :] = lax.dot_general(
            scaled, b, TN, preferred_element_type=F32
        ).astype(BF16)


def block_work(conv_input, rim8, conv_weight, conv_bias, cl_g, clt, dtt, end_g, skip, inner, nstate):
    rows, dim = conv_input.shape[1:]
    taps = conv_weight.shape[0]
    wide = inner // GROUPS
    per = cl_g.shape[2]
    first_b = inner // nstate
    first_c = first_b + GROUPS
    bias = conv_bias[None, :]

    def three(lead, block_rows):
        zero = (0,) * len(lead)
        return [
            pl.BlockSpec(lead + (block_rows, wide), lambda g: zero + (0, g)),
            pl.BlockSpec(lead + (block_rows, nstate), lambda g: zero + (0, first_b + g)),
            pl.BlockSpec(lead + (block_rows, nstate), lambda g: zero + (0, first_c + g)),
        ]

    by_group = pl.BlockSpec((1, rows, per), lambda g: (g, 0, 0))
    by_rows = pl.BlockSpec((per, rows), lambda g: (g, 0))
    return pl.pallas_call(
        block_kernel,
        grid=(GROUPS,),
        in_specs=three((1,), rows)
        + three((), 8)
        + three((), taps)
        + three((), 1)
        + [by_group, by_rows, by_rows, by_group, pl.BlockSpec((1, wide), lambda g: (0, g))],
        out_specs=[
            pl.BlockSpec((rows, wide), lambda g: (0, g)),
            pl.BlockSpec((wide, nstate), lambda g: (g, 0)),
            pl.BlockSpec((rows, nstate), lambda g: (0, g)),
        ],
        out_shape=[
            jax.ShapeDtypeStruct((rows, inner), F32),
            jax.ShapeDtypeStruct((inner, nstate), BF16),
            jax.ShapeDtypeStruct((rows, GROUPS * nstate), BF16),
        ],
        scratch_shapes=[pltpu.VMEM((rows + 8, wide + 2 * nstate), F32)],
        compiler_params=params(32),
        cost_estimate=cost(30 * 10**9, 40 * 2**20),
        name="block_work",
    )(
        *([conv_input] * 3), *([rim8] * 3), *([conv_weight] * 3), *([bias] * 3),
        cl_g, clt, dtt, end_g, skip,
    )


def finish_kernel(count, y, c, rst, cl, gate, gain, out, g_ref):
    rows, wide = y.shape
    grown = jnp.exp(cl[0])
    left = lax.broadcasted_iota(jnp.int32, (rows, 128), 1) < 64
    squares = jnp.zeros((rows, 128), F32)
    for pair in range(wide // 128):
        cols = slice(pair * 128, pair * 128 + 128)
        carried = lax.dot_general(c[...], rst[cols, :], NT, preferred_element_type=F32)
        growth = jnp.where(left, grown[:, 2 * pair : 2 * pair + 1], grown[:, 2 * pair + 1 : 2 * pair + 2])
        g = (y[:, cols] + carried * growth) * jax.nn.silu(gate[0, :, cols].astype(F32))
        g_ref[:, cols] = g
        squares = squares + g * g
    mean = jnp.sum(squares, axis=1, keepdims=True) / wide
    live = lax.broadcasted_iota(jnp.int32, (rows, 1), 0) < count[0]
    factor = jnp.where(live, lax.rsqrt(mean + 1e-05), 0.0)
    for pair in range(wide // 128):
        cols = slice(pair * 128, pair * 128 + 128)
        out[0, :, cols] = (g_ref[:, cols] * factor * gain[:, cols]).astype(BF16)


def finish(count, y, c, rst, cl_g, gate, gain):
    rows, inner = y.shape
    wide = inner // GROUPS
    nstate = rst.shape[1]
    per = cl_g.shape[2]
    return pl.pallas_call(
        finish_kernel,
        grid_spec=pltpu.PrefetchScalarGridSpec(
            num_scalar_prefetch=1,
            grid=(GROUPS,),
            in_specs=[
                pl.BlockSpec((rows, wide), lambda g, s: (0, g)),
                pl.BlockSpec((rows, nstate), lambda g, s: (0, g)),
                pl.BlockSpec((wide, nstate), lambda g, s: (g, 0)),
                pl.BlockSpec((1, rows, per), lambda g, s: (g, 0, 0)),
                pl.BlockSpec((1, rows, wide), lambda g, s: (0, 0, g)),
                pl.BlockSpec((1, wide), lambda g, s: (0, g)),
            ],
            out_specs=pl.BlockSpec((1, rows, wide), lambda g, s: (0, 0, g)),
            scratch_shapes=[pltpu.VMEM((rows, wide), F32)],
        ),
        out_shape=jax.ShapeDtypeStruct((1, rows, inner), BF16),
        compiler_params=params(32),
        cost_estimate=cost(10 * 10**9, 40 * 2**20),
        name="finish",
    )(count, y, c, rst, cl_g, gate, gain)


def combine_kernel(pages, scale_a, scale_b, a, b, out):
    _, page_rows, _ = out.shape
    width = a.shape[0] // scale_a.shape[0]
    per = page_rows // width

    def one(i, carry):
        page = pages[pl.program_id(0) * out.shape[0] + i]
        for h in range(per):
            head = page * per + h
            rows = pl.ds(pl.multiple_of(head * width, width), width)
            total = a[rows, :].astype(F32) * scale_a[head] + b[rows, :].astype(F32) * scale_b[head]
            out[i, h * width : (h + 1) * width, :] = total.astype(BF16)
        return carry

    lax.fori_loop(0, out.shape[0], one, 0)


def combine(pages, scale_a, scale_b, a, b, page_rows):
    devices = pages.shape[0]
    nstate = a.shape[1]
    steps = 2
    whole = pl.BlockSpec(a.shape, lambda i, *s: (0, 0))
    return pl.pallas_call(
        combine_kernel,
        grid_spec=pltpu.PrefetchScalarGridSpec(
            num_scalar_prefetch=3,
            grid=(steps,),
            in_specs=[whole, whole],
            out_specs=pl.BlockSpec((devices // steps, page_rows, nstate), lambda i, *s: (i, 0, 0)),
        ),
        out_shape=jax.ShapeDtypeStruct((devices, page_rows, nstate), BF16),
        compiler_params=params(32),
        cost_estimate=cost(0, 6 * 2**20),
        name="combine",
    )(pages, scale_a, scale_b, a, b)


def store_kernel(source, used, decay, pool, back, out):
    slots, page_rows, _ = out.shape
    per = decay.shape[1]
    width = page_rows // per

    def one(i, carry):
        slot = pl.program_id(0) * slots + i
        for h in range(per):
            rows = slice(h * width, (h + 1) * width)
            part = back[source[slot], rows, :].astype(F32)
            part = jnp.where(used[slot] > 0, part, 0.0)
            out[i, rows, :] = pool[i, rows, :] * decay[slot, h] + part
        return carry

    lax.fori_loop(0, slots, one, 0)


def store_pages(source, used, decay, pool, back):
    slots, page_rows, nstate = pool.shape
    steps = 4
    block = pl.BlockSpec((slots // steps, page_rows, nstate), lambda i, *s: (i, 0, 0))
    return pl.pallas_call(
        store_kernel,
        grid_spec=pltpu.PrefetchScalarGridSpec(
            num_scalar_prefetch=3,
            grid=(steps,),
            in_specs=[block, pl.BlockSpec(back.shape, lambda i, *s: (0, 0, 0))],
            out_specs=block,
        ),
        out_shape=jax.ShapeDtypeStruct(pool.shape, F32),
        compiler_params=params(32),
        cost_estimate=cost(0, 10 * 2**20),
        name="store_pages",
    )(source, used, decay, pool, back)


def local(
    conv_input,
    gate_input,
    dt_raw,
    conv_weight,
    conv_bias,
    dt_bias,
    a_log,
    d_skip,
    norm_weight,
    conv_cache,
    state_pool,
    page_owner,
    page_slot,
    prefix_len,
    new_count,
):
    req_count = lax.axis_size("req")
    ctx_count = lax.axis_size("ctx")
    devices = req_count * ctx_count
    req_index = lax.axis_index("req")
    ctx_index = lax.axis_index("ctx")
    own_index = req_index * ctx_count + ctx_index
    swap = [(0, 1), (1, 0)]
    tokens = conv_input[0]
    rows = tokens.shape[0]
    heads = dt_raw.shape[2]
    inner = gate_input.shape[2]
    width = inner // heads
    pool_slots, page_rows, nstate = state_pool.shape
    device_pages = page_owner.shape[1] // ctx_count
    page_heads = page_rows // width
    rim = conv_weight.shape[0] - 1
    per_group = heads // GROUPS
    prefix = prefix_len[req_index]
    count = new_count[req_index]
    owner_table = page_owner.reshape(devices, device_pages)
    slot_table = page_slot.reshape(devices, device_pages)
    page_ids = jnp.arange(device_pages, dtype=jnp.int32)
    matches = owner_table == own_index
    slot_for = jnp.sum(jnp.where(matches, slot_table, 0), axis=1)
    page_for = jnp.sum(jnp.where(matches, page_ids[None, :], 0), axis=1)
    present = jnp.any(matches, axis=1)
    incoming = lax.all_to_all(
        fetch_pages(state_pool, slot_for), ("req", "ctx"), split_axis=0, concat_axis=0, tiled=True
    )
    my_owners = owner_table[own_index]

    previous = lax.ppermute(tokens[rows - rim :], "ctx", [(0, 1)])
    keep_rows = jnp.arange(rim) >= rim - prefix
    cached = jnp.where(keep_rows[:, None], conv_cache[0], jnp.zeros_like(conv_cache[0]))
    rim_rows = jnp.where(ctx_index == 0, cached, previous)
    rim8 = jnp.concatenate([jnp.zeros((8 - rim, tokens.shape[1]), F32), rim_rows.astype(F32)], axis=0)

    positions = ctx_index * rows + jnp.arange(rows)
    live = positions < count
    step_size = jax.nn.softplus(dt_raw[0].astype(F32) + dt_bias) * live[:, None].astype(F32)
    cumulative = jnp.cumsum(step_size * -jnp.exp(a_log), axis=0)
    ending = jnp.exp(cumulative[-1][None, :] - cumulative) * step_size
    all_ends = jnp.exp(lax.all_gather(cumulative[-1], ("req", "ctx"), axis=0))
    by_request = all_ends.reshape(req_count, ctx_count, heads)

    def grouped(array):
        return jnp.moveaxis(array.reshape(rows, GROUPS, per_group), 1, 0)

    cl_g = grouped(cumulative)
    y, states, c_proj = block_work(
        conv_input, rim8, conv_weight, conv_bias, cl_g, cumulative.T, step_size.T,
        grouped(ending), jnp.repeat(d_skip, width)[None, :], inner, nstate,
    )

    share = inner // ctx_count
    head_share = heads // ctx_count
    mine = lax.dynamic_slice_in_dim(states, ctx_index * share, share, 0)
    theirs = lax.dynamic_slice_in_dim(states, (1 - ctx_index) * share, share, 0)
    other = lax.ppermute(theirs, "ctx", swap)
    later = lax.dynamic_slice_in_dim(by_request[req_index, 1], ctx_index * head_share, head_share, 0)
    ones = jnp.ones_like(later)
    outbound = combine(
        jnp.sum(
            jnp.where(my_owners[None, :] == jnp.arange(devices)[:, None], page_ids[None, :], 0), axis=1
        ),
        jnp.where(ctx_index == 0, later, ones),
        jnp.where(ctx_index == 0, ones, later),
        mine,
        other,
        page_rows,
    )
    returned = lax.all_to_all(outbound, ("req", "ctx"), split_axis=0, concat_axis=0, tiled=True)

    first_half = lax.ppermute(states[:share], "ctx", [(0, 1)])
    before = jnp.concatenate([first_half, jnp.where(ctx_index == 0, jnp.zeros_like(other), other)], axis=0)
    initial = lax.all_gather(incoming[my_owners].reshape(share, nstate), "ctx", axis=0, tiled=True)
    factor = jnp.where(ctx_index == 0, 1.0, by_request[req_index, 0]) * (prefix > 0).astype(F32)
    start = (
        initial.astype(F32).reshape(heads, width, nstate) * factor[:, None, None]
        + before.astype(F32).reshape(heads, width, nstate)
    ).astype(BF16)
    mixed = finish(
        (count - ctx_index * rows).reshape(1),
        y, c_proj, start.reshape(inner, nstate), cl_g, gate_input, norm_weight[None, :],
    )

    targets = count - rim + jnp.arange(rim) - ctx_index * rows
    inside = (targets >= 0) & (targets < rows)
    tail = jnp.where(inside[:, None], tokens[jnp.clip(targets, 0, rows - 1)], jnp.zeros((), BF16))
    new_tail = tail + lax.ppermute(tail, "ctx", swap)

    total = jnp.prod(by_request, axis=1) * (prefix_len > 0).astype(F32)[:, None]
    paged = total.reshape(devices, device_pages, page_heads)
    chosen = (page_for[:, None] == page_ids[None, :])[:, :, None]
    page_decay = jnp.sum(jnp.where(chosen, paged, 0.0), axis=1)
    hit = (slot_for[None, :] == jnp.arange(pool_slots)[:, None]) & present[None, :]
    used = jnp.any(hit, axis=1)
    source = jnp.sum(jnp.where(hit, jnp.arange(devices, dtype=jnp.int32)[None, :], 0), axis=1)
    slot_decay = jnp.sum(jnp.where(hit[:, :, None], page_decay[None], 0.0), axis=1)
    slot_decay = jnp.where(used[:, None], slot_decay, 1.0)
    new_pool = store_pages(source, used.astype(jnp.int32), slot_decay, state_pool, returned)
    return (mixed, new_tail[None], new_pool)


def solution(mesh):
    return jax.shard_map(
        local,
        mesh=mesh,
        in_specs=(
            P("req", "ctx", None),
            P("req", "ctx", None),
            P("req", "ctx", None),
            P(),
            P(),
            P(),
            P(),
            P(),
            P(),
            P("req", None, None),
            P(("req", "ctx"), None, None),
            P(),
            P(),
            P(),
            P(),
        ),
        out_specs=(P("req", "ctx", None), P("req", None, None), P(("req", "ctx"), None, None)),
        check_vma=False,
    )
```

```python
import jax
import jax.numpy as jnp
from jax import lax
from jax.experimental import pallas as pl
from jax.experimental.pallas import tpu as pltpu
from jax.sharding import PartitionSpec as P

GROUPS = 8
F32 = jnp.float32
BF16 = jnp.bfloat16
NT = (((1,), (1,)), ((), ()))
TN = (((0,), (0,)), ((), ()))


def params(mib):
    return pltpu.CompilerParams(vmem_limit_bytes=mib * 1024 * 1024)


def cost(flops, moved):
    return pl.CostEstimate(flops=flops, bytes_accessed=moved, transcendentals=0)


def fetch_kernel(slots, pool, out, held, sems):
    count = out.shape[0]

    def copy(i):
        return pltpu.make_async_copy(pool.at[slots[i]], held.at[i], sems.at[i])

    def begin(i, carry):
        copy(i).start()
        return carry

    def one(i, carry):
        copy(i).wait()
        out[i] = held[i].astype(BF16)
        return carry

    lax.fori_loop(0, count, begin, 0)
    lax.fori_loop(0, count, one, 0)


def fetch_pages(pool, slots):
    shape = (slots.shape[0],) + pool.shape[1:]
    return pl.pallas_call(
        fetch_kernel,
        grid_spec=pltpu.PrefetchScalarGridSpec(
            num_scalar_prefetch=1,
            grid=(1,),
            in_specs=[pl.BlockSpec(memory_space=pltpu.HBM)],
            out_specs=pl.BlockSpec(shape, lambda i, s: (0, 0, 0)),
            scratch_shapes=[pltpu.VMEM(shape, F32), pltpu.SemaphoreType.DMA((shape[0],))],
        ),
        out_shape=jax.ShapeDtypeStruct(shape, BF16),
        compiler_params=params(32),
        cost_estimate=cost(0, 6 * 2**20),
        name="fetch_pages",
    )(slots, pool)


def block_kernel(
    xin, bin_, cin, rimx, rimb, rimc, wx, wb, wc, ax, ab, ac, cl, clt, dtt, end, skip,
    y_ref, st_ref, c_ref, ext,
):
    rows, wide = xin.shape[1:]
    nstate = bin_.shape[2]
    taps = wx.shape[0]
    pad = rimx.shape[0]
    half = rows // 2
    for at, body, rim in ((0, xin, rimx), (wide, bin_, rimb), (wide + nstate, cin, rimc)):
        size = body.shape[2]
        ext[0:pad, at : at + size] = rim[...]
        ext[pad : pad + rows, at : at + size] = body[0].astype(F32)

    def act(at, col, size, weight, bias):
        accum = jnp.broadcast_to(bias[:, col : col + size], (rows, size))
        for k in range(taps):
            start = pad - taps + 1 + k
            piece = ext[start : start + rows, at + col : at + col + size]
            accum = accum + weight[k : k + 1, col : col + size] * piece
        return jax.nn.silu(accum).astype(BF16)

    b = act(wide, 0, nstate, wb, ab)
    c = act(wide + nstate, 0, nstate, wc, ac)
    c_ref[...] = c
    scores = lax.dot_general(c, b, NT, preferred_element_type=F32)
    row_id = lax.broadcasted_iota(jnp.int32, (half, half), 0)
    col_id = lax.broadcasted_iota(jnp.int32, (half, half), 1)
    lower = row_id >= col_id
    left = lax.broadcasted_iota(jnp.int32, (half, 128), 1) < 64
    left_all = lax.broadcasted_iota(jnp.int32, (rows, 128), 1) < 64
    for pair in range(wide // 128):
        cols = slice(pair * 128, pair * 128 + 128)
        x = act(0, pair * 128, 128, wx, ax)
        xf = x.astype(F32)
        tops, bottoms = [], []
        for head in (2 * pair, 2 * pair + 1):
            down = cl[0, :, head : head + 1]
            across = clt[head : head + 1, :]
            dt = dtt[head : head + 1, :]

            def part(r, s, diagonal):
                gap = down[r * half : (r + 1) * half] - across[:, s * half : (s + 1) * half]
                if diagonal:
                    gap = jnp.where(lower, gap, -1e30)
                value = scores[r * half : (r + 1) * half, s * half : (s + 1) * half] * jnp.exp(gap)
                return (value * dt[:, s * half : (s + 1) * half]).astype(BF16)

            tops.append(jnp.dot(part(0, 0, True), x[:half], preferred_element_type=F32))
            low = jnp.concatenate([part(1, 0, False), part(1, 1, True)], axis=1)
            bottoms.append(jnp.dot(low, x, preferred_element_type=F32))
        y_ref[0:half, cols] = jnp.where(left, tops[0], tops[1]) + skip[:, cols] * xf[:half]
        y_ref[half:rows, cols] = jnp.where(left, bottoms[0], bottoms[1]) + skip[:, cols] * xf[half:]
        ending = jnp.where(
            left_all, end[0, :, 2 * pair : 2 * pair + 1], end[0, :, 2 * pair + 1 : 2 * pair + 2]
        )
        scaled = (xf * ending).astype(BF16)
        st_ref[pair * 128 : pair * 128 + 128, :] = lax.dot_general(
            scaled, b, TN, preferred_element_type=F32
        ).astype(BF16)


def block_work(conv_input, rim8, conv_weight, conv_bias, cl_g, clt, dtt, end_g, skip, inner, nstate):
    rows, dim = conv_input.shape[1:]
    taps = conv_weight.shape[0]
    wide = inner // GROUPS
    per = cl_g.shape[2]
    first_b = inner // nstate
    first_c = first_b + GROUPS
    bias = conv_bias[None, :]

    def three(lead, block_rows):
        zero = (0,) * len(lead)
        return [
            pl.BlockSpec(lead + (block_rows, wide), lambda g: zero + (0, g)),
            pl.BlockSpec(lead + (block_rows, nstate), lambda g: zero + (0, first_b + g)),
            pl.BlockSpec(lead + (block_rows, nstate), lambda g: zero + (0, first_c + g)),
        ]

    by_group = pl.BlockSpec((1, rows, per), lambda g: (g, 0, 0))
    by_rows = pl.BlockSpec((per, rows), lambda g: (g, 0))
    return pl.pallas_call(
        block_kernel,
        grid=(GROUPS,),
        in_specs=three((1,), rows)
        + three((), 8)
        + three((), taps)
        + three((), 1)
        + [by_group, by_rows, by_rows, by_group, pl.BlockSpec((1, wide), lambda g: (0, g))],
        out_specs=[
            pl.BlockSpec((rows, wide), lambda g: (0, g)),
            pl.BlockSpec((wide, nstate), lambda g: (g, 0)),
            pl.BlockSpec((rows, nstate), lambda g: (0, g)),
        ],
        out_shape=[
            jax.ShapeDtypeStruct((rows, inner), F32),
            jax.ShapeDtypeStruct((inner, nstate), BF16),
            jax.ShapeDtypeStruct((rows, GROUPS * nstate), BF16),
        ],
        scratch_shapes=[pltpu.VMEM((rows + 8, wide + 2 * nstate), F32)],
        compiler_params=params(32),
        cost_estimate=cost(30 * 10**9, 40 * 2**20),
        name="block_work",
    )(
        *([conv_input] * 3), *([rim8] * 3), *([conv_weight] * 3), *([bias] * 3),
        cl_g, clt, dtt, end_g, skip,
    )


def finish_kernel(count, y, c, rst, cl, gate, gain, out, g_ref):
    rows, wide = y.shape
    grown = jnp.exp(cl[0])
    left = lax.broadcasted_iota(jnp.int32, (rows, 128), 1) < 64
    squares = jnp.zeros((rows, 128), F32)
    for pair in range(wide // 128):
        cols = slice(pair * 128, pair * 128 + 128)
        carried = lax.dot_general(c[...], rst[cols, :], NT, preferred_element_type=F32)
        growth = jnp.where(left, grown[:, 2 * pair : 2 * pair + 1], grown[:, 2 * pair + 1 : 2 * pair + 2])
        g = (y[:, cols] + carried * growth) * jax.nn.silu(gate[0, :, cols].astype(F32))
        g_ref[:, cols] = g
        squares = squares + g * g
    mean = jnp.sum(squares, axis=1, keepdims=True) / wide
    live = lax.broadcasted_iota(jnp.int32, (rows, 1), 0) < count[0]
    factor = jnp.where(live, lax.rsqrt(mean + 1e-05), 0.0)
    for pair in range(wide // 128):
        cols = slice(pair * 128, pair * 128 + 128)
        out[0, :, cols] = (g_ref[:, cols] * factor * gain[:, cols]).astype(BF16)


def finish(count, y, c, rst, cl_g, gate, gain):
    rows, inner = y.shape
    wide = inner // GROUPS
    nstate = rst.shape[1]
    per = cl_g.shape[2]
    return pl.pallas_call(
        finish_kernel,
        grid_spec=pltpu.PrefetchScalarGridSpec(
            num_scalar_prefetch=1,
            grid=(GROUPS,),
            in_specs=[
                pl.BlockSpec((rows, wide), lambda g, s: (0, g)),
                pl.BlockSpec((rows, nstate), lambda g, s: (0, g)),
                pl.BlockSpec((wide, nstate), lambda g, s: (g, 0)),
                pl.BlockSpec((1, rows, per), lambda g, s: (g, 0, 0)),
                pl.BlockSpec((1, rows, wide), lambda g, s: (0, 0, g)),
                pl.BlockSpec((1, wide), lambda g, s: (0, g)),
            ],
            out_specs=pl.BlockSpec((1, rows, wide), lambda g, s: (0, 0, g)),
            scratch_shapes=[pltpu.VMEM((rows, wide), F32)],
        ),
        out_shape=jax.ShapeDtypeStruct((1, rows, inner), BF16),
        compiler_params=params(32),
        cost_estimate=cost(10 * 10**9, 40 * 2**20),
        name="finish",
    )(count, y, c, rst, cl_g, gate, gain)


def combine_kernel(pages, scale_a, scale_b, scale_old, a, b, old, out):
    _, page_rows, _ = out.shape
    width = a.shape[0] // scale_a.shape[0]
    per = page_rows // width

    def one(i, carry):
        page = pages[pl.program_id(0) * out.shape[0] + i]
        for h in range(per):
            head = page * per + h
            rows = pl.ds(pl.multiple_of(head * width, width), width)
            at = slice(h * width, (h + 1) * width)
            total = a[rows, :].astype(F32) * scale_a[head] + b[rows, :].astype(F32) * scale_b[head]
            out[i, at, :] = (total + old[i, at, :].astype(F32) * scale_old[head]).astype(BF16)
        return carry

    lax.fori_loop(0, out.shape[0], one, 0)


def combine(pages, scale_a, scale_b, scale_old, a, b, old):
    devices, page_rows, nstate = old.shape
    steps = 2
    whole = pl.BlockSpec(a.shape, lambda i, *s: (0, 0))
    paged = pl.BlockSpec((devices // steps, page_rows, nstate), lambda i, *s: (i, 0, 0))
    return pl.pallas_call(
        combine_kernel,
        grid_spec=pltpu.PrefetchScalarGridSpec(
            num_scalar_prefetch=4,
            grid=(steps,),
            in_specs=[whole, whole, paged],
            out_specs=paged,
        ),
        out_shape=jax.ShapeDtypeStruct(old.shape, BF16),
        compiler_params=params(32),
        cost_estimate=cost(0, 6 * 2**20),
        name="combine",
    )(pages, scale_a, scale_b, scale_old, a, b, old)


def store_kernel(source, used, pool, back, after, out):
    slots = out.shape[0]

    def one(i, carry):
        slot = pl.program_id(0) * slots + i

        @pl.when(used[slot] > 0)
        def _():
            out[i] = back[source[slot]].astype(F32)

        @pl.when(used[slot] == 0)
        def _():
            out[i] = pool[i]

        return carry

    lax.fori_loop(0, slots, one, 0)


def store_pages(source, used, pool, back, after):
    slots, page_rows, nstate = pool.shape
    steps = 4
    block = pl.BlockSpec((slots // steps, page_rows, nstate), lambda i, *s: (i, 0, 0))
    return pl.pallas_call(
        store_kernel,
        grid_spec=pltpu.PrefetchScalarGridSpec(
            num_scalar_prefetch=2,
            grid=(steps,),
            in_specs=[
                block,
                pl.BlockSpec(back.shape, lambda i, *s: (0, 0, 0)),
                pl.BlockSpec(memory_space=pltpu.HBM),
            ],
            out_specs=block,
        ),
        out_shape=jax.ShapeDtypeStruct(pool.shape, F32),
        compiler_params=params(32),
        cost_estimate=cost(0, 10 * 2**20),
        name="store_pages",
    )(source, used, pool, back, after)


def local(
    conv_input,
    gate_input,
    dt_raw,
    conv_weight,
    conv_bias,
    dt_bias,
    a_log,
    d_skip,
    norm_weight,
    conv_cache,
    state_pool,
    page_owner,
    page_slot,
    prefix_len,
    new_count,
):
    req_count = lax.axis_size("req")
    ctx_count = lax.axis_size("ctx")
    devices = req_count * ctx_count
    req_index = lax.axis_index("req")
    ctx_index = lax.axis_index("ctx")
    own_index = req_index * ctx_count + ctx_index
    swap = [(0, 1), (1, 0)]
    tokens = conv_input[0]
    rows = tokens.shape[0]
    heads = dt_raw.shape[2]
    inner = gate_input.shape[2]
    width = inner // heads
    pool_slots, page_rows, nstate = state_pool.shape
    device_pages = page_owner.shape[1] // ctx_count
    rim = conv_weight.shape[0] - 1
    per_group = heads // GROUPS
    prefix = prefix_len[req_index]
    count = new_count[req_index]
    owner_table = page_owner.reshape(devices, device_pages)
    slot_table = page_slot.reshape(devices, device_pages)
    page_ids = jnp.arange(device_pages, dtype=jnp.int32)
    matches = owner_table == own_index
    slot_for = jnp.sum(jnp.where(matches, slot_table, 0), axis=1)
    present = jnp.any(matches, axis=1)
    fetched, edge = lax.optimization_barrier(
        (fetch_pages(state_pool, slot_for), tokens[rows - (conv_weight.shape[0] - 1) :])
    )
    incoming = lax.all_to_all(fetched, ("req", "ctx"), split_axis=0, concat_axis=0, tiled=True)
    my_owners = owner_table[own_index]

    previous = lax.ppermute(edge, "ctx", [(0, 1)])
    keep_rows = jnp.arange(rim) >= rim - prefix
    cached = jnp.where(keep_rows[:, None], conv_cache[0], jnp.zeros_like(conv_cache[0]))
    rim_rows = jnp.where(ctx_index == 0, cached, previous)
    rim8 = jnp.concatenate([jnp.zeros((8 - rim, tokens.shape[1]), F32), rim_rows.astype(F32)], axis=0)

    positions = ctx_index * rows + jnp.arange(rows)
    live = positions < count
    step_size = jax.nn.softplus(dt_raw[0].astype(F32) + dt_bias) * live[:, None].astype(F32)
    cumulative = jnp.cumsum(step_size * -jnp.exp(a_log), axis=0)
    ending = jnp.exp(cumulative[-1][None, :] - cumulative) * step_size
    own_decay = jnp.exp(cumulative[-1])
    other_decay = lax.ppermute(own_decay, "ctx", swap)
    is_first = ctx_index == 0
    decay_first = jnp.where(is_first, own_decay, other_decay)
    decay_later = jnp.where(is_first, other_decay, own_decay)
    resumed = (prefix > 0).astype(F32)

    def grouped(array):
        return jnp.moveaxis(array.reshape(rows, GROUPS, per_group), 1, 0)

    cl_g = grouped(cumulative)
    y, states, c_proj = block_work(
        conv_input, rim8, conv_weight, conv_bias, cl_g, cumulative.T, step_size.T,
        grouped(ending), jnp.repeat(d_skip, width)[None, :], inner, nstate,
    )

    share = inner // ctx_count
    head_share = heads // ctx_count
    mine = lax.dynamic_slice_in_dim(states, ctx_index * share, share, 0)
    theirs = lax.dynamic_slice_in_dim(states, (1 - ctx_index) * share, share, 0)
    other = lax.ppermute(theirs, "ctx", swap)
    later = lax.dynamic_slice_in_dim(decay_later, ctx_index * head_share, head_share, 0)
    whole = lax.dynamic_slice_in_dim(decay_first * decay_later * resumed, ctx_index * head_share, head_share, 0)
    ones = jnp.ones_like(later)
    targets = count - rim + jnp.arange(rim) - ctx_index * rows
    outbound, targets, arrived = lax.optimization_barrier((
        combine(
            jnp.sum(
                jnp.where(my_owners[None, :] == jnp.arange(devices)[:, None], page_ids[None, :], 0), axis=1
            ),
            jnp.where(is_first, later, ones),
            jnp.where(is_first, ones, later),
            whole,
            mine,
            other,
            incoming,
        ),
        targets,
        incoming,
    ))
    returned = lax.all_to_all(outbound, ("req", "ctx"), split_axis=0, concat_axis=0, tiled=True)

    first_half = lax.ppermute(states[:share], "ctx", [(0, 1)])
    before = jnp.concatenate([first_half, jnp.where(is_first, jnp.zeros_like(other), other)], axis=0)
    old = arrived[my_owners].reshape(share, nstate)
    old_other = lax.ppermute(old, "ctx", swap)
    initial = jnp.concatenate(
        [jnp.where(is_first, old, old_other), jnp.where(is_first, old_other, old)], axis=0
    )
    factor = jnp.where(is_first, 1.0, decay_first) * resumed
    start = (
        initial.astype(F32).reshape(heads, width, nstate) * factor[:, None, None]
        + before.astype(F32).reshape(heads, width, nstate)
    ).astype(BF16)
    mixed = finish(
        (count - ctx_index * rows).reshape(1),
        y, c_proj, start.reshape(inner, nstate), cl_g, gate_input, norm_weight[None, :],
    )

    inside = (targets >= 0) & (targets < rows)
    tail = jnp.where(inside[:, None], tokens[jnp.clip(targets, 0, rows - 1)], jnp.zeros((), BF16))
    new_tail = tail + lax.ppermute(tail, "ctx", swap)

    hit = (slot_for[None, :] == jnp.arange(pool_slots)[:, None]) & present[None, :]
    used = jnp.any(hit, axis=1)
    source = jnp.sum(jnp.where(hit, jnp.arange(devices, dtype=jnp.int32)[None, :], 0), axis=1)
    new_pool = store_pages(source, used.astype(jnp.int32), state_pool, returned, mixed)
    return (mixed, new_tail[None], new_pool)


def solution(mesh):
    return jax.shard_map(
        local,
        mesh=mesh,
        in_specs=(
            P("req", "ctx", None),
            P("req", "ctx", None),
            P("req", "ctx", None),
            P(),
            P(),
            P(),
            P(),
            P(),
            P(),
            P("req", None, None),
            P(("req", "ctx"), None, None),
            P(),
            P(),
            P(),
            P(),
        ),
        out_specs=(P("req", "ctx", None), P("req", None, None), P(("req", "ctx"), None, None)),
        check_vma=False,
    )
```

```python
import jax
import jax.numpy as jnp
from jax import lax
from jax.experimental import pallas as pl
from jax.experimental.pallas import tpu as pltpu
from jax.sharding import PartitionSpec as P

GROUPS = 8
F32 = jnp.float32
BF16 = jnp.bfloat16
NT = (((1,), (1,)), ((), ()))
TN = (((0,), (0,)), ((), ()))


def params(mib):
    return pltpu.CompilerParams(vmem_limit_bytes=mib * 1024 * 1024)


def cost(flops, moved):
    return pl.CostEstimate(flops=flops, bytes_accessed=moved, transcendentals=0)


def fetch_kernel(slots, pool, out, held, sems):
    count = out.shape[0]

    def copy(i):
        return pltpu.make_async_copy(pool.at[slots[i]], held.at[i], sems.at[i])

    def begin(i, carry):
        copy(i).start()
        return carry

    def one(i, carry):
        copy(i).wait()
        out[i] = held[i].astype(BF16)
        return carry

    lax.fori_loop(0, count, begin, 0)
    lax.fori_loop(0, count, one, 0)


def fetch_pages(pool, slots):
    shape = (slots.shape[0],) + pool.shape[1:]
    return pl.pallas_call(
        fetch_kernel,
        grid_spec=pltpu.PrefetchScalarGridSpec(
            num_scalar_prefetch=1,
            grid=(1,),
            in_specs=[pl.BlockSpec(memory_space=pltpu.HBM)],
            out_specs=pl.BlockSpec(shape, lambda i, s: (0, 0, 0)),
            scratch_shapes=[pltpu.VMEM(shape, F32), pltpu.SemaphoreType.DMA((shape[0],))],
        ),
        out_shape=jax.ShapeDtypeStruct(shape, BF16),
        compiler_params=params(58),
        cost_estimate=cost(0, 6 * 2**20),
        name="fetch_pages",
    )(slots, pool)


def block_kernel(
    xin, bin_, cin, rimx, rimb, rimc, wx, wb, wc, ax, ab, ac, cl, clt, dtt, end, skip,
    y_ref, st_ref, c_ref, ext,
):
    rows, wide = xin.shape[1:]
    nstate = bin_.shape[2]
    taps = wx.shape[0]
    pad = rimx.shape[0]
    half = rows // 2
    for at, body, rim in ((0, xin, rimx), (wide, bin_, rimb), (wide + nstate, cin, rimc)):
        size = body.shape[2]
        ext[0:pad, at : at + size] = rim[...]
        ext[pad : pad + rows, at : at + size] = body[0].astype(F32)

    def act(at, col, size, weight, bias):
        accum = jnp.broadcast_to(bias[:, col : col + size], (rows, size))
        for k in range(taps):
            start = pad - taps + 1 + k
            piece = ext[start : start + rows, at + col : at + col + size]
            accum = accum + weight[k : k + 1, col : col + size] * piece
        return jax.nn.silu(accum).astype(BF16)

    b = act(wide, 0, nstate, wb, ab)
    c = act(wide + nstate, 0, nstate, wc, ac)
    c_ref[...] = c
    scores = lax.dot_general(c, b, NT, preferred_element_type=F32)
    row_id = lax.broadcasted_iota(jnp.int32, (half, half), 0)
    col_id = lax.broadcasted_iota(jnp.int32, (half, half), 1)
    lower = row_id >= col_id
    left = lax.broadcasted_iota(jnp.int32, (half, 128), 1) < 64
    left_all = lax.broadcasted_iota(jnp.int32, (rows, 128), 1) < 64
    for pair in range(wide // 128):
        cols = slice(pair * 128, pair * 128 + 128)
        x = act(0, pair * 128, 128, wx, ax)
        xf = x.astype(F32)
        tops, bottoms = [], []
        for head in (2 * pair, 2 * pair + 1):
            down = cl[0, :, head : head + 1]
            across = clt[head : head + 1, :]
            dt = dtt[head : head + 1, :]

            def part(r, s, diagonal):
                gap = down[r * half : (r + 1) * half] - across[:, s * half : (s + 1) * half]
                if diagonal:
                    gap = jnp.where(lower, gap, -1e30)
                value = scores[r * half : (r + 1) * half, s * half : (s + 1) * half] * jnp.exp(gap)
                return (value * dt[:, s * half : (s + 1) * half]).astype(BF16)

            tops.append(jnp.dot(part(0, 0, True), x[:half], preferred_element_type=F32))
            low = jnp.concatenate([part(1, 0, False), part(1, 1, True)], axis=1)
            bottoms.append(jnp.dot(low, x, preferred_element_type=F32))
        y_ref[0:half, cols] = jnp.where(left, tops[0], tops[1]) + skip[:, cols] * xf[:half]
        y_ref[half:rows, cols] = jnp.where(left, bottoms[0], bottoms[1]) + skip[:, cols] * xf[half:]
        ending = jnp.where(
            left_all, end[0, :, 2 * pair : 2 * pair + 1], end[0, :, 2 * pair + 1 : 2 * pair + 2]
        )
        scaled = (xf * ending).astype(BF16)
        st_ref[pair * 128 : pair * 128 + 128, :] = lax.dot_general(
            scaled, b, TN, preferred_element_type=F32
        ).astype(BF16)


def block_work(conv_input, rim8, conv_weight, conv_bias, cl_g, clt, dtt, end_g, skip, inner, nstate):
    rows, dim = conv_input.shape[1:]
    taps = conv_weight.shape[0]
    wide = inner // GROUPS
    per = cl_g.shape[2]
    first_b = inner // nstate
    first_c = first_b + GROUPS
    bias = conv_bias[None, :]

    def three(lead, block_rows):
        zero = (0,) * len(lead)
        return [
            pl.BlockSpec(lead + (block_rows, wide), lambda g: zero + (0, g)),
            pl.BlockSpec(lead + (block_rows, nstate), lambda g: zero + (0, first_b + g)),
            pl.BlockSpec(lead + (block_rows, nstate), lambda g: zero + (0, first_c + g)),
        ]

    by_group = pl.BlockSpec((1, rows, per), lambda g: (g, 0, 0))
    by_rows = pl.BlockSpec((per, rows), lambda g: (g, 0))
    return pl.pallas_call(
        block_kernel,
        grid=(GROUPS,),
        in_specs=three((1,), rows)
        + three((), 8)
        + three((), taps)
        + three((), 1)
        + [by_group, by_rows, by_rows, by_group, pl.BlockSpec((1, wide), lambda g: (0, g))],
        out_specs=[
            pl.BlockSpec((rows, wide), lambda g: (0, g)),
            pl.BlockSpec((wide, nstate), lambda g: (g, 0)),
            pl.BlockSpec((rows, nstate), lambda g: (0, g)),
        ],
        out_shape=[
            jax.ShapeDtypeStruct((rows, inner), F32),
            jax.ShapeDtypeStruct((inner, nstate), BF16),
            jax.ShapeDtypeStruct((rows, GROUPS * nstate), BF16),
        ],
        scratch_shapes=[pltpu.VMEM((rows + 8, wide + 2 * nstate), F32)],
        compiler_params=params(58),
        cost_estimate=cost(1000, 1000),
        name="block_work",
    )(
        *([conv_input] * 3), *([rim8] * 3), *([conv_weight] * 3), *([bias] * 3),
        cl_g, clt, dtt, end_g, skip,
    )


def finish_kernel(count, y, c, rst, cl, gate, gain, out, g_ref):
    rows, wide = y.shape
    grown = jnp.exp(cl[0])
    left = lax.broadcasted_iota(jnp.int32, (rows, 128), 1) < 64
    squares = jnp.zeros((rows, 128), F32)
    for pair in range(wide // 128):
        cols = slice(pair * 128, pair * 128 + 128)
        carried = lax.dot_general(c[...], rst[cols, :], NT, preferred_element_type=F32)
        growth = jnp.where(left, grown[:, 2 * pair : 2 * pair + 1], grown[:, 2 * pair + 1 : 2 * pair + 2])
        g = (y[:, cols] + carried * growth) * jax.nn.silu(gate[0, :, cols].astype(F32))
        g_ref[:, cols] = g
        squares = squares + g * g
    mean = jnp.sum(squares, axis=1, keepdims=True) / wide
    live = lax.broadcasted_iota(jnp.int32, (rows, 1), 0) < count[0]
    factor = jnp.where(live, lax.rsqrt(mean + 1e-05), 0.0)
    for pair in range(wide // 128):
        cols = slice(pair * 128, pair * 128 + 128)
        out[0, :, cols] = (g_ref[:, cols] * factor * gain[:, cols]).astype(BF16)


def finish(count, y, c, rst, cl_g, gate, gain):
    rows, inner = y.shape
    wide = inner // GROUPS
    nstate = rst.shape[1]
    per = cl_g.shape[2]
    return pl.pallas_call(
        finish_kernel,
        grid_spec=pltpu.PrefetchScalarGridSpec(
            num_scalar_prefetch=1,
            grid=(GROUPS,),
            in_specs=[
                pl.BlockSpec((rows, wide), lambda g, s: (0, g)),
                pl.BlockSpec((rows, nstate), lambda g, s: (0, g)),
                pl.BlockSpec((wide, nstate), lambda g, s: (g, 0)),
                pl.BlockSpec((1, rows, per), lambda g, s: (g, 0, 0)),
                pl.BlockSpec((1, rows, wide), lambda g, s: (0, 0, g)),
                pl.BlockSpec((1, wide), lambda g, s: (0, g)),
            ],
            out_specs=pl.BlockSpec((1, rows, wide), lambda g, s: (0, 0, g)),
            scratch_shapes=[pltpu.VMEM((rows, wide), F32)],
        ),
        out_shape=jax.ShapeDtypeStruct((1, rows, inner), BF16),
        compiler_params=params(58),
        cost_estimate=cost(1000, 1000),
        name="finish",
    )(count, y, c, rst, cl_g, gate, gain)


def combine_kernel(pages, scale_a, scale_b, scale_old, which, a, b, old, out):
    _, page_rows, _ = out.shape
    width = a.shape[0] // scale_a.shape[0]
    per = page_rows // width

    def one(i, carry):
        page = pages[pl.program_id(0) * out.shape[0] + i]
        for h in range(per):
            head = page * per + h
            rows = pl.ds(pl.multiple_of(head * width, width), width)
            at = slice(h * width, (h + 1) * width)
            total = a[rows, :].astype(F32) * scale_a[head] + b[rows, :].astype(F32) * scale_b[head]
            out[i, at, :] = (total + old[i, at, :].astype(F32) * scale_old[head]).astype(BF16)
        return carry

    lax.fori_loop(0, out.shape[0], one, 0)


def combine(pages, scale_a, scale_b, scale_old, which, a, b, old):
    devices, page_rows, nstate = old.shape
    steps = 2
    own = pl.BlockSpec(b.shape, lambda i, *s: (s[4][0], 0))
    whole = pl.BlockSpec(b.shape, lambda i, *s: (0, 0))
    paged = pl.BlockSpec((devices // steps, page_rows, nstate), lambda i, *s: (i, 0, 0))
    return pl.pallas_call(
        combine_kernel,
        grid_spec=pltpu.PrefetchScalarGridSpec(
            num_scalar_prefetch=5,
            grid=(steps,),
            in_specs=[own, whole, paged],
            out_specs=paged,
        ),
        out_shape=jax.ShapeDtypeStruct(old.shape, BF16),
        compiler_params=params(32),
        cost_estimate=cost(0, 6 * 2**20),
        name="combine",
    )(pages, scale_a, scale_b, scale_old, which, a, b, old)


def store_kernel(source, used, pool, back, after, out):
    slots = out.shape[0]

    def one(i, carry):
        slot = pl.program_id(0) * slots + i

        @pl.when(used[slot] > 0)
        def _():
            out[i] = back[source[slot]].astype(F32)

        @pl.when(used[slot] == 0)
        def _():
            out[i] = pool[i]

        return carry

    lax.fori_loop(0, slots, one, 0)


def store_pages(source, used, pool, back, after):
    slots, page_rows, nstate = pool.shape
    steps = 4
    block = pl.BlockSpec((slots // steps, page_rows, nstate), lambda i, *s: (i, 0, 0))
    return pl.pallas_call(
        store_kernel,
        grid_spec=pltpu.PrefetchScalarGridSpec(
            num_scalar_prefetch=2,
            grid=(steps,),
            in_specs=[
                block,
                pl.BlockSpec(back.shape, lambda i, *s: (0, 0, 0)),
                pl.BlockSpec(memory_space=pltpu.HBM),
            ],
            out_specs=block,
        ),
        out_shape=jax.ShapeDtypeStruct(pool.shape, F32),
        compiler_params=params(58),
        cost_estimate=cost(0, 10 * 2**20),
        name="store_pages",
    )(source, used, pool, back, after)


def local(
    conv_input,
    gate_input,
    dt_raw,
    conv_weight,
    conv_bias,
    dt_bias,
    a_log,
    d_skip,
    norm_weight,
    conv_cache,
    state_pool,
    page_owner,
    page_slot,
    prefix_len,
    new_count,
):
    req_count = lax.axis_size("req")
    ctx_count = lax.axis_size("ctx")
    devices = req_count * ctx_count
    req_index = lax.axis_index("req")
    ctx_index = lax.axis_index("ctx")
    own_index = req_index * ctx_count + ctx_index
    swap = [(0, 1), (1, 0)]
    tokens = conv_input[0]
    rows = tokens.shape[0]
    heads = dt_raw.shape[2]
    inner = gate_input.shape[2]
    width = inner // heads
    pool_slots, page_rows, nstate = state_pool.shape
    device_pages = page_owner.shape[1] // ctx_count
    rim = conv_weight.shape[0] - 1
    per_group = heads // GROUPS
    prefix = prefix_len[req_index]
    count = new_count[req_index]
    owner_table = page_owner.reshape(devices, device_pages)
    slot_table = page_slot.reshape(devices, device_pages)
    page_ids = jnp.arange(device_pages, dtype=jnp.int32)
    matches = owner_table == own_index
    slot_for = jnp.sum(jnp.where(matches, slot_table, 0), axis=1)
    present = jnp.any(matches, axis=1)
    fetched, edge = lax.optimization_barrier(
        (fetch_pages(state_pool, slot_for), tokens[rows - (conv_weight.shape[0] - 1) :])
    )
    incoming = lax.all_to_all(fetched, ("req", "ctx"), split_axis=0, concat_axis=0, tiled=True)
    my_owners = owner_table[own_index]

    previous = lax.ppermute(edge, "ctx", [(0, 1)])
    keep_rows = jnp.arange(rim) >= rim - prefix
    cached = jnp.where(keep_rows[:, None], conv_cache[0], jnp.zeros_like(conv_cache[0]))
    rim_rows = jnp.where(ctx_index == 0, cached, previous)
    rim8 = jnp.concatenate([jnp.zeros((8 - rim, tokens.shape[1]), F32), rim_rows.astype(F32)], axis=0)

    positions = ctx_index * rows + jnp.arange(rows)
    live = positions < count
    step_size = jax.nn.softplus(dt_raw[0].astype(F32) + dt_bias) * live[:, None].astype(F32)
    cumulative = jnp.cumsum(step_size * -jnp.exp(a_log), axis=0)
    ending = jnp.exp(cumulative[-1][None, :] - cumulative) * step_size
    own_decay = jnp.exp(cumulative[-1])
    other_decay = lax.ppermute(own_decay, "ctx", swap)
    is_first = ctx_index == 0
    decay_first = jnp.where(is_first, own_decay, other_decay)
    decay_later = jnp.where(is_first, other_decay, own_decay)
    resumed = (prefix > 0).astype(F32)

    def grouped(array):
        return jnp.moveaxis(array.reshape(rows, GROUPS, per_group), 1, 0)

    cl_g = grouped(cumulative)
    y, states, c_proj = block_work(
        conv_input, rim8, conv_weight, conv_bias, cl_g, cumulative.T, step_size.T,
        grouped(ending), jnp.repeat(d_skip, width)[None, :], inner, nstate,
    )

    share = inner // ctx_count
    head_share = heads // ctx_count
    theirs = lax.dynamic_slice_in_dim(states, (1 - ctx_index) * share, share, 0)
    other = lax.ppermute(theirs, "ctx", swap)
    later = lax.dynamic_slice_in_dim(decay_later, ctx_index * head_share, head_share, 0)
    whole = lax.dynamic_slice_in_dim(decay_first * decay_later * resumed, ctx_index * head_share, head_share, 0)
    ones = jnp.ones_like(later)
    targets = count - rim + jnp.arange(rim) - ctx_index * rows
    outbound, targets, arrived = lax.optimization_barrier((
        combine(
            jnp.sum(
                jnp.where(my_owners[None, :] == jnp.arange(devices)[:, None], page_ids[None, :], 0), axis=1
            ),
            jnp.where(is_first, later, ones),
            jnp.where(is_first, ones, later),
            whole,
            ctx_index.reshape(1),
            states,
            other,
            incoming,
        ),
        targets,
        incoming,
    ))
    returned = lax.all_to_all(outbound, ("req", "ctx"), split_axis=0, concat_axis=0, tiled=True)

    first_half = lax.ppermute(states[:share], "ctx", [(0, 1)])
    before = jnp.concatenate([first_half, jnp.where(is_first, jnp.zeros_like(other), other)], axis=0)
    old = arrived[my_owners].reshape(share, nstate)
    old_other = lax.ppermute(old, "ctx", swap)
    initial = jnp.concatenate(
        [jnp.where(is_first, old, old_other), jnp.where(is_first, old_other, old)], axis=0
    )
    factor = jnp.where(is_first, 1.0, decay_first) * resumed
    start = (
        initial.astype(F32).reshape(heads, width, nstate) * factor[:, None, None]
        + before.astype(F32).reshape(heads, width, nstate)
    ).astype(BF16)
    mixed = finish(
        (count - ctx_index * rows).reshape(1),
        y, c_proj, start.reshape(inner, nstate), cl_g, gate_input, norm_weight[None, :],
    )

    inside = (targets >= 0) & (targets < rows)
    tail = jnp.where(inside[:, None], tokens[jnp.clip(targets, 0, rows - 1)], jnp.zeros((), BF16))
    new_tail = tail + lax.ppermute(tail, "ctx", swap)

    hit = (slot_for[None, :] == jnp.arange(pool_slots)[:, None]) & present[None, :]
    used = jnp.any(hit, axis=1)
    source = jnp.sum(jnp.where(hit, jnp.arange(devices, dtype=jnp.int32)[None, :], 0), axis=1)
    new_pool = store_pages(source, used.astype(jnp.int32), state_pool, returned, mixed)
    return (mixed, new_tail[None], new_pool)


def solution(mesh):
    return jax.shard_map(
        local,
        mesh=mesh,
        in_specs=(
            P("req", "ctx", None),
            P("req", "ctx", None),
            P("req", "ctx", None),
            P(),
            P(),
            P(),
            P(),
            P(),
            P(),
            P("req", None, None),
            P(("req", "ctx"), None, None),
            P(),
            P(),
            P(),
            P(),
        ),
        out_specs=(P("req", "ctx", None), P("req", None, None), P(("req", "ctx"), None, None)),
        check_vma=False,
    )
```
